256 devices in a mesh: dp: 32 (over x_hi, z, core), expert: 8 (over x_lo, y).
Axes of the slice: x: 4 (x_hi: 2, x_lo: 2; x = x_hi * 2 + x_lo), y: 4, z: 8, core: 2. Of those that a mesh axis runs over, the one named last changes fastest.
Arguments:
- tokens: bfloat16 [49152, 2048], P(('dp', 'expert')), may hold values from -6 to 6
- routes: int32 [49152, 2], P(('dp', 'expert')), may hold values from 0 to 7, all different within a row; in each aligned block of 192 rows (0 to 191, 192 to 383, ...) at most 60 rows name the same one
- route_weights: float32 [49152, 2], P(('dp', 'expert')), may hold values from 0.2 to 1
- cotangent: bfloat16 [49152, 2048], P(('dp', 'expert')), may hold values from -0.75 to 0.75
- w_gate: bfloat16 [8, 2048, 768], P('expert', 'dp'), may hold values from -0.125 to 0.125
- w_up: bfloat16 [8, 2048, 768], P('expert', 'dp'), may hold values from -0.125 to 0.125
- w_down: bfloat16 [8, 768, 2048], P('expert', 'dp'), may hold values from -0.21875 to 0.21875
Outputs:
- mixed: bfloat16 [49152, 2048], P(('dp', 'expert'))
- token_grad: bfloat16 [49152, 2048], P(('dp', 'expert'))
- grad_gate: bfloat16 [8, 2048, 768], P('expert', 'dp')
- grad_up: bfloat16 [8, 2048, 768], P('expert', 'dp')
- grad_down: bfloat16 [8, 768, 2048], P('expert', 'dp')
The draws below stay inside these ranges and needn't reach their ends.
Inputs may be any that keep to these rules, and one draw needn't show every extreme that they name: Each token names 2 different experts; within the 192 tokens of one device no expert is named by more than 60 routes, a bound that some block reaches.
All inputs are finite; a program needn't handle non-finite values.
Results may differ from the reference program's by a relative error of at most 0.02.
Values may be sent and summed in bfloat16 or wider, within the bound.
No kernel may reach another device: no remote copies, remote signals or barrier semaphores. Data moves between devices by JAX's collectives and lax.ppermute only.
A program may use at most 128 MiB of HBM per device.

```python
import math
import jax
import jax.numpy as jnp
import numpy as np
from jax import lax

D = 2048
FF = 768
EXPERTS = 8
TOP = 2
TOK_DEV = 192
CAP = 60
TOKENS = 49152
N_DP = 32
N_EXPERT = 8


def block_levels(stream_key, extent, split, smallest, high):
    def one(position, blocks):
        heights = jax.random.uniform(jax.random.fold_in(jax.random.fold_in(stream_key, 6), position), (blocks,), jnp.float32, smallest / len(split), high / len(split))
        return jnp.repeat(jnp.exp(heights), extent[position] // blocks).reshape((-1,) + (1,) * (len(extent) - position - 1))

    factor_of = one(*split[0])
    for cut in split[1:]:
        factor_of = factor_of * one(*cut)
    return factor_of


def deal_out(own_key, own, number, rows, amount, top, reach, lean):
    ranking = jax.random.permutation(own_key, amount)
    packed, common = load_shares(amount, rows * top, reach, lean, True), load_shares(amount, rows * top, reach, lean, False)
    places = jnp.arange(amount)

    def named(lengths, rotation):
        used = int((lengths > 0).sum())
        fixed = max(1, used // 4)
        passed = fixed + (places - fixed + rotation * (used - fixed)) % max(1, amount - fixed)
        return jnp.zeros((amount,), jnp.int32).at[ranking[jnp.where(places < fixed, places, passed)]].set(jnp.asarray(lengths, jnp.int32))

    lengths = jnp.where(number % 4 == 0, named(packed, number // 4), named(common, number - number // 4 - 1))
    mixed = jax.random.permutation(jax.random.fold_in(own, 3), amount)
    giver, taker = mixed[0:amount // 2 * 2:2], mixed[1:amount // 2 * 2:2]
    slack = jnp.minimum(lengths[giver] - 1, reach - lengths[taker]) // 2
    slack = jnp.where((giver == ranking[0]) | (taker == ranking[0]) | (lengths[taker] == 0), 0, jnp.maximum(slack, 0))
    passed = jax.random.randint(jax.random.fold_in(own, 4), (amount // 2,), 0, 1 << 20) % (slack + 1)
    lengths = lengths.at[giver].add(-passed).at[taker].add(passed)
    labels = jnp.searchsorted(jnp.cumsum(lengths), jnp.arange(rows * top), side="right").astype(jnp.int32)
    grid = labels.reshape(top, rows).T
    grid = grid[jax.random.permutation(jax.random.fold_in(own, 1), rows)]
    rotation = jax.random.randint(jax.random.fold_in(own, 2), (rows, 1), 0, top)
    return jnp.take_along_axis(grid, (jnp.arange(top)[None, :] + rotation) % top, axis=1)


def load_shares(amount, total, bound, skew, full):
    portions = [(1 << 20) // math.isqrt(grade ** skew) + 1 for grade in range(1, amount + 1)]
    largest = bound if full else min(bound, max(-(-total // amount), total * portions[0] // sum(portions)))
    least = 1 if total - largest >= amount - 1 else 0
    holding, spare = [largest] + [least] * (amount - 1), total - largest - least * (amount - 1)
    while spare > 0:
        candidates = [i for i in range(1, amount) if holding[i] < largest] or [i for i in range(1, amount) if holding[i] < bound]
        whole, left = sum([portions[i] for i in candidates]), spare
        for i in candidates:
            more = min(bound - holding[i], max(1, left * portions[i] // whole), spare)
            holding[i] = holding[i] + more
            spare = spare - more
    return np.array(holding)


def bell_draw(rng, shape, scale, bound, cuts=(), held_as=jnp.bfloat16):
    array = jax.random.normal(rng, shape, jnp.float32) * scale
    if len(cuts) > 0:
        array = block_levels(rng, shape, cuts, -0.22, 0.18) * array
    return jnp.clip(array, min=-bound, max=bound).astype(held_as)


def setup_inputs(seed: int = 0) -> dict:
    key_of = jax.random.split(jax.random.key(seed), 8)
    tokens = bell_draw(key_of[0], (TOKENS, D), 1.0, 6.0, ((0, 256),))
    routes_keys = jax.random.split(jax.random.fold_in(key_of[1], 1), TOKENS // TOK_DEV)
    routes_turns = jax.random.permutation(jax.random.fold_in(key_of[1], 3), TOKENS // TOK_DEV)
    routes = jax.vmap(lambda own, number: deal_out(jax.random.fold_in(key_of[1], 2), own, number, TOK_DEV, EXPERTS, TOP, CAP, 1))(routes_keys, routes_turns).reshape((TOKENS, TOP))
    route_weights = jnp.clip(0.2 + 0.8 * jax.random.uniform(key_of[2], (TOKENS, TOP), jnp.float32) ** block_levels(key_of[2], (TOKENS, TOP), ((0, 256),), -0.2, 0.2), 0.2, 1.0)
    cotangent = bell_draw(key_of[3], (TOKENS, D), 0.125, 0.75, ((0, 256),))
    w_gate = bell_draw(key_of[4], (EXPERTS, D, FF), D ** -0.5, 0.125, ((0, 8), (1, 32)))
    w_up = bell_draw(key_of[5], (EXPERTS, D, FF), D ** -0.5, 0.125, ((0, 8), (1, 32)))
    w_down = bell_draw(key_of[6], (EXPERTS, FF, D), FF ** -0.5, 0.21875, ((0, 8), (1, 32)))
    return {"tokens": tokens, "routes": routes, "route_weights": route_weights, "cotangent": cotangent, "w_gate": w_gate, "w_up": w_up, "w_down": w_down}


highest = lax.Precision.HIGHEST


def slot_numbers(route_ids):
    onehot = (route_ids[..., None] == jnp.arange(EXPERTS, dtype=jnp.int32)).astype(jnp.int32)
    before = jnp.cumsum(onehot, axis=-2) - onehot
    return jnp.sum(before * onehot, axis=-1).astype(jnp.int32)


def reference(tokens, routes, route_weights, cotangent, w_gate, w_up, w_down):
    sources = N_EXPERT
    per_block = TOK_DEV * TOP
    slots_all = EXPERTS * CAP
    tok_blocks = tokens.reshape(N_DP, sources, TOK_DEV, D)
    route_blocks = routes.reshape(N_DP, sources, per_block)
    weight_blocks = route_weights.reshape(N_DP, sources, TOK_DEV, TOP)
    cot_blocks = cotangent.reshape(N_DP, sources, TOK_DEV, D)
    gate_full = w_gate.astype(jnp.float32)
    up_full = w_up.astype(jnp.float32)
    down_full = w_down.astype(jnp.float32)

    def one_group(totals, inputs):
        tok_block, route_block, weight_block, cot_block = inputs
        target = (route_block * CAP + slot_numbers(route_block)).astype(jnp.int32)
        routing_table = (jnp.arange(slots_all, dtype=jnp.int32)[None, :, None] == target[:, None, :]).astype(jnp.float32)
        token_table = jnp.sum(routing_table.reshape(sources, slots_all, TOK_DEV, TOP), axis=3)
        sent_rows = jnp.einsum('set,std->sed', token_table, tok_block.astype(jnp.float32), precision=highest).astype(jnp.bfloat16)
        scaled = (weight_block[..., None] * cot_block[:, :, None, :].astype(jnp.float32)).astype(jnp.bfloat16)
        sent_grads = jnp.einsum('ser,srd->sed', routing_table, scaled.reshape(sources, per_block, D).astype(jnp.float32), precision=highest).astype(jnp.bfloat16)
        rows_in = sent_rows.reshape(sources, EXPERTS, CAP, D).astype(jnp.float32)
        grads_in = sent_grads.reshape(sources, EXPERTS, CAP, D).astype(jnp.float32)
        gate_values = jnp.einsum('secd,edf->secf', rows_in, gate_full, precision=highest)
        up_values = jnp.einsum('secd,edf->secf', rows_in, up_full, precision=highest)
        sigmoid_gate = jax.nn.sigmoid(gate_values)
        hidden = (gate_values * sigmoid_gate * up_values).astype(jnp.bfloat16)
        output = jnp.einsum('secf,efd->secd', hidden.astype(jnp.float32), down_full, precision=highest).astype(jnp.bfloat16)
        picked = jnp.take_along_axis(output.reshape(sources, slots_all, D), target[..., None], axis=1)
        picked = picked.reshape(sources, TOK_DEV, TOP, D)
        mixed = jnp.sum(weight_block[..., None] * picked.astype(jnp.float32), axis=2).astype(jnp.bfloat16)
        hidden_grad = jnp.einsum('secd,efd->secf', grads_in, down_full, precision=highest)
        gate_grad = (hidden_grad * up_values * sigmoid_gate * (1.0 + gate_values * (1.0 - sigmoid_gate))).astype(jnp.bfloat16)
        up_grad = (hidden_grad * gate_values * sigmoid_gate).astype(jnp.bfloat16)
        input_grad = jnp.einsum('secf,edf->secd', gate_grad.astype(jnp.float32), gate_full, precision=highest)
        input_grad = input_grad + jnp.einsum('secf,edf->secd', up_grad.astype(jnp.float32), up_full, precision=highest)
        input_grad = input_grad.astype(jnp.bfloat16)
        picked_grad = jnp.take_along_axis(input_grad.reshape(sources, slots_all, D), target[..., None], axis=1)
        token_grad = jnp.sum(picked_grad.reshape(sources, TOK_DEV, TOP, D).astype(jnp.float32), axis=2).astype(jnp.bfloat16)
        partial_gate = jnp.einsum('secd,secf->edf', rows_in, gate_grad.astype(jnp.float32), precision=highest)
        partial_up = jnp.einsum('secd,secf->edf', rows_in, up_grad.astype(jnp.float32), precision=highest)
        partial_down = jnp.einsum('secf,secd->efd', hidden.astype(jnp.float32), grads_in, precision=highest)
        rounded = lax.optimization_barrier((partial_gate.astype(jnp.bfloat16), partial_up.astype(jnp.bfloat16), partial_down.astype(jnp.bfloat16)))
        totals = (totals[0] + rounded[0].astype(jnp.float32), totals[1] + rounded[1].astype(jnp.float32), totals[2] + rounded[2].astype(jnp.float32))
        return totals, (mixed, token_grad)

    initial = (jnp.zeros((EXPERTS, D, FF), jnp.float32), jnp.zeros((EXPERTS, D, FF), jnp.float32), jnp.zeros((EXPERTS, FF, D), jnp.float32))
    totals, outputs = lax.scan(one_group, initial, (tok_blocks, route_blocks, weight_blocks, cot_blocks))
    mixed = outputs[0].reshape(TOKENS, D)
    token_grad = outputs[1].reshape(TOKENS, D)
    return mixed, token_grad, totals[0].astype(jnp.bfloat16), totals[1].astype(jnp.bfloat16), totals[2].astype(jnp.bfloat16)
```

```python
import jax
import jax.numpy as jnp
from jax import lax
from jax.sharding import PartitionSpec as P

EXPERTS = 8
CAP = 60
N_X, N_Z, N_C = 2, 8, 2
N_L, N_Y = 2, 4
BF = jnp.bfloat16
F32 = jnp.float32


def dp_index(x, z, c):
    return (x * N_Z + z) * N_C + c


DP_ALL = [(x, z, c) for x in range(N_X) for z in range(N_Z) for c in range(N_C)]
PERM_UP = [(dp_index(x, z, c), dp_index(x, (z + 1) % N_Z, c)) for x, z, c in DP_ALL]
PERM_DOWN = [(dp_index(x, z, c), dp_index(x, (z - 1) % N_Z, c)) for x, z, c in DP_ALL]
PERM_CORE = [(dp_index(x, z, c), dp_index(x, z, 1 - c)) for x, z, c in DP_ALL]
PERM_X = [(dp_index(x, z, c), dp_index(1 - x, z, c)) for x, z, c in DP_ALL]
PERM_X_TO = [(dp_index(c, z, c), dp_index(1 - c, z, c)) for z in range(N_Z) for c in range(N_C)]
PERM_X_FROM = [(b, a) for a, b in PERM_X_TO]
PERM_CORE_FROM = [(dp_index(c, z, c), dp_index(c, z, 1 - c)) for z in range(N_Z) for c in range(N_C)]
PERM_L = [(a * N_Y + y, (1 - a) * N_Y + y) for a in range(N_L) for y in range(N_Y)]


def perm_y(shift):
    return [(a * N_Y + y, a * N_Y + (y + shift) % N_Y) for a in range(N_L) for y in range(N_Y)]


def over_dp(value, perm):
    return lax.ppermute(value, "dp", perm)


def over_expert(value, perm):
    return lax.ppermute(value, "expert", perm)


def mm(a, b, dims=((1,), (0,))):
    return lax.dot_general(a, b, (dims, ((), ())), preferred_element_type=F32)


def put(buffer, part, z, row=0):
    return lax.dynamic_update_slice(buffer, part[None], (z, row, 0))


def ring_gather(slab, z):
    rows = slab.shape[0]
    half = rows // 2
    buffer = put(jnp.zeros((N_Z,) + slab.shape, slab.dtype), slab, z)
    up, down = slab, slab
    for step in range(1, 4):
        up, down = over_dp(up, PERM_UP), over_dp(down, PERM_DOWN)
        buffer = put(buffer, up, (z - step) % N_Z)
        buffer = put(buffer, down, (z + step) % N_Z)
    up, down = over_dp(up[:half], PERM_UP), over_dp(down[half:], PERM_DOWN)
    buffer = put(buffer, up, (z + 4) % N_Z)
    return put(buffer, down, (z + 4) % N_Z, half)


def ring_scatter(partial, z):
    rows = partial.shape[1]
    half = rows // 2

    def at(step):
        return lax.dynamic_index_in_dim(partial, (z + step) % N_Z, 0, keepdims=False)

    far = at(4)
    up, down = over_dp(far[:half], PERM_UP), over_dp(far[half:], PERM_DOWN)
    near_up, near_down = at(3), at(5)
    up = jnp.concatenate([near_up[:half] + up, near_up[half:]], axis=0)
    down = jnp.concatenate([near_down[:half], near_down[half:] + down], axis=0)
    up, down = over_dp(up, PERM_UP), over_dp(down, PERM_DOWN)
    for step in (2, 1):
        up, down = over_dp(at(step) + up, PERM_UP), over_dp(at(-step) + down, PERM_DOWN)
    return at(0).astype(F32) + up.astype(F32) + down.astype(F32)


def pick(first, a, b, axis):
    return jnp.where(first, jnp.concatenate([a, b], axis=axis), jnp.concatenate([b, a], axis=axis))


def send_blocks(rows):
    n = rows.shape[0] // N_Y
    got = [rows[:n]] + [over_expert(rows[k * n : (k + 1) * n], perm_y(k)) for k in range(1, N_Y)]
    return jnp.concatenate(got, axis=0)


def return_blocks(rows):
    n = rows.shape[0] // N_Y
    got = [rows[:n]] + [over_expert(rows[k * n : (k + 1) * n], perm_y(-k)) for k in range(1, N_Y)]
    return jnp.concatenate(got, axis=0)


def slots_of(routes):
    tok_rows = routes.shape[0]
    experts = jnp.arange(EXPERTS, dtype=jnp.int32)
    onehot = (routes[:, :, None] == experts).astype(F32)
    named = jnp.sum(onehot, axis=1).astype(BF)
    earlier = jnp.arange(tok_rows)[:, None] > jnp.arange(tok_rows)[None, :]
    before = mm(earlier.astype(BF), named)
    return jnp.sum(onehot * before[:, None, :], axis=2)


def shards(tokens, routes, route_weights, cotangent, w_gate, w_up, w_down):
    tok_rows, width = tokens.shape
    ff = w_gate.shape[2]
    half_ff = ff // 2
    half_d = width // 2
    dp = lax.axis_index("dp")
    expert = lax.axis_index("expert")
    c, z, x = dp % N_C, (dp // N_C) % N_Z, dp // (N_C * N_Z)
    y, low = expert % N_Y, expert // N_Y
    on_c0, on_x0 = c == 0, x == 0

    packed = jnp.concatenate(
        [routes.astype(F32).T, slots_of(routes).T, route_weights.T], axis=0
    )
    packed_peer = over_expert(packed, PERM_L)
    tokens_peer = over_expert(tokens, PERM_L)
    cot_peer = over_expert(cotangent, PERM_L)

    wg, wu, wd = w_gate[0], w_up[0], w_down[0]

    def halves(k):
        return jnp.concatenate(
            [
                lax.dynamic_slice_in_dim(wg, k * half_ff, half_ff, 1),
                lax.dynamic_slice_in_dim(wu, k * half_ff, half_ff, 1),
            ],
            axis=1,
        )

    near = pick(on_c0, halves(c), over_dp(halves(1 - c), PERM_CORE), 0)
    far = over_dp(near, PERM_X)
    down_pair = pick(on_c0, wd, over_dp(wd, PERM_CORE), 0)
    down_slab = jnp.where(x == c, down_pair, over_dp(down_pair, PERM_X_TO))

    near_own = ring_gather(near, z).reshape(half_d, ff)
    far_own = ring_gather(far, z).reshape(half_d, ff)
    down_own = ring_gather(down_slab, z).reshape(half_ff, width)
    near_oth = over_dp(near_own, PERM_CORE)
    far_oth = over_dp(far_own, PERM_CORE)
    down_oth = over_dp(down_own, PERM_CORE)

    both = jnp.concatenate([packed, packed_peer], axis=1)
    source = (jnp.arange(2 * tok_rows) >= tok_rows).astype(jnp.int32) * CAP
    slot_rows = N_Y * 2 * CAP
    numbers = jnp.arange(slot_rows, dtype=jnp.int32)[:, None]
    table = jnp.zeros((slot_rows, 2 * tok_rows), F32)
    weight_table = jnp.zeros((slot_rows, 2 * tok_rows), F32)
    for j in range(2):
        ids = both[j].astype(jnp.int32)
        row = ((ids % N_Y - y) % N_Y) * (2 * CAP) + source + both[2 + j].astype(jnp.int32)
        row = jnp.where(ids // N_Y == low, row, -1)
        hit = numbers == row[None, :]
        table = table + hit.astype(F32)
        weight_table = weight_table + jnp.where(hit, both[4 + j][None, :], 0.0)
    table = table.astype(BF)
    weight_hi = weight_table.astype(BF)
    weight_lo = (weight_table - weight_hi.astype(F32)).astype(BF)
    slot_weight = jnp.sum(weight_table, axis=1, keepdims=True)

    def swapped(values):
        return pick(on_x0, values[:, :half_d], values[:, half_d:], 1)

    sent_rows = mm(table, jnp.concatenate([swapped(tokens), swapped(tokens_peer)], axis=0)).astype(BF)
    rows = send_blocks(sent_rows)
    sent_grads = mm(table, jnp.concatenate([cotangent, cot_peer], axis=0))
    grads = send_blocks((sent_grads * slot_weight).astype(BF))

    rows_near, rows_far = rows[:, :half_d], rows[:, half_d:]

    def forward(w_near, w_far):
        both_values = mm(rows_near, w_near) + mm(rows_far, w_far)
        gate, up = both_values[:, :half_ff], both_values[:, half_ff:]
        sig = jax.nn.sigmoid(gate)
        return gate, up, sig, (gate * sig * up).astype(BF)

    gate_own, up_own, sig_own, hid_own = forward(near_own, far_own)
    gate_oth, up_oth, sig_oth, hid_oth = forward(near_oth, far_oth)

    def backward(gate, up, sig, w):
        hidden_grad = mm(grads, w, ((1,), (1,)))
        gate_grad = hidden_grad * up * sig * (1.0 + gate * (1.0 - sig))
        up_grad = hidden_grad * gate * sig
        return jnp.concatenate([gate_grad.astype(BF), up_grad.astype(BF)], axis=1)

    grad_own = backward(gate_own, up_own, sig_own, down_own)
    grad_oth = backward(gate_oth, up_oth, sig_oth, down_oth)

    def partial(a, own, oth, shape):
        mine = mm(a, own, ((0,), (0,))).astype(BF)
        theirs = over_dp(mm(a, oth, ((0,), (0,))).astype(BF), PERM_CORE)
        return (mine + theirs).reshape(shape)

    gu_shape = (N_Z, half_d // N_Z, ff)
    mine = mm(hid_own, grads, ((0,), (0,))).astype(BF)
    theirs = over_dp(mm(hid_oth, grads, ((0,), (0,))).astype(BF), PERM_CORE)
    part_down = (mine + theirs).reshape(N_Z, half_ff // N_Z, width)
    part_far = partial(rows_far, grad_own, grad_oth, gu_shape)
    part_near = partial(rows_near, grad_own, grad_oth, gu_shape)

    output = (mm(hid_own, down_own) + mm(hid_oth, down_oth)).astype(BF)
    returned = return_blocks(output)

    def input_grad(w_own, w_oth):
        return (mm(grad_own, w_own, ((1,), (1,))) + mm(grad_oth, w_oth, ((1,), (1,)))).astype(BF)

    grad_back = return_blocks(
        jnp.concatenate([input_grad(near_own, near_oth), input_grad(far_own, far_oth)], axis=1)
    )

    sum_down = ring_scatter(part_down, z)
    sum_far = ring_scatter(part_far, z)
    sum_near = ring_scatter(part_near, z)

    def combine(tables, values):
        def part(lo, hi):
            return sum(mm(t[:, lo:hi], values, ((0,), (0,))) for t in tables)

        peer = over_expert(part(tok_rows, 2 * tok_rows).astype(BF), PERM_L)
        return (part(0, tok_rows) + peer.astype(F32)).astype(BF)

    mixed = combine((weight_hi, weight_lo), returned)
    token_grad = swapped(combine((table,), grad_back))

    gu = (sum_near + over_dp(sum_far.astype(BF), PERM_X).astype(F32)).astype(BF)
    part_rows = gu.shape[0] // 2
    keep = lax.dynamic_slice_in_dim(gu, c * part_rows, part_rows, 0)
    give = lax.dynamic_slice_in_dim(gu, (1 - c) * part_rows, part_rows, 0)
    took = over_dp(give, PERM_CORE)
    grad_gate = pick(on_c0, keep[:, :half_ff], took[:, :half_ff], 1)
    grad_up = pick(on_c0, keep[:, half_ff:], took[:, half_ff:], 1)

    down = (sum_down + over_dp(sum_down.astype(BF), PERM_X_FROM).astype(F32)).astype(BF)
    part_rows = down.shape[0] // 2
    keep = lax.dynamic_slice_in_dim(down, c * part_rows, part_rows, 0)
    give = lax.dynamic_slice_in_dim(down, (1 - c) * part_rows, part_rows, 0)
    grad_down = jnp.where(x == c, keep, over_dp(give, PERM_CORE_FROM))

    return mixed, token_grad, grad_gate[None], grad_up[None], grad_down[None]


def solution(mesh):
    in_specs = (
        P(("dp", "expert"), None),
        P(("dp", "expert"), None),
        P(("dp", "expert"), None),
        P(("dp", "expert"), None),
        P("expert", "dp", None),
        P("expert", "dp", None),
        P("expert", "dp", None),
    )
    out_specs = (
        P(("dp", "expert"), None),
        P(("dp", "expert"), None),
        P("expert", "dp", None),
        P("expert", "dp", None),
        P("expert", "dp", None),
    )
    return jax.shard_map(shards, mesh=mesh, in_specs=in_specs, out_specs=out_specs, check_vma=False)
```

```python
import jax
import jax.numpy as jnp
from jax import lax
from jax.sharding import PartitionSpec as P

EXPERTS = 8
BLOCK = 64
N_X, N_Z, N_C = 2, 8, 2
N_L, N_Y = 2, 4
BF = jnp.bfloat16
F32 = jnp.float32


def dp_index(x, z, c):
    return (x * N_Z + z) * N_C + c


DP_ALL = [(x, z, c) for x in range(N_X) for z in range(N_Z) for c in range(N_C)]
PERM_UP = [(dp_index(x, z, c), dp_index(x, (z + 1) % N_Z, c)) for x, z, c in DP_ALL]
PERM_DOWN = [(dp_index(x, z, c), dp_index(x, (z - 1) % N_Z, c)) for x, z, c in DP_ALL]
PERM_CORE = [(dp_index(x, z, c), dp_index(x, z, 1 - c)) for x, z, c in DP_ALL]
PERM_X = [(dp_index(x, z, c), dp_index(1 - x, z, c)) for x, z, c in DP_ALL]
PERM_X_TO = [(dp_index(c, z, c), dp_index(1 - c, z, c)) for z in range(N_Z) for c in range(N_C)]
PERM_L = [(a * N_Y + y, (1 - a) * N_Y + y) for a in range(N_L) for y in range(N_Y)]


def perm_y(shift):
    return [(a * N_Y + y, a * N_Y + (y + shift) % N_Y) for a in range(N_L) for y in range(N_Y)]


def over_dp(value, perm):
    return lax.ppermute(value, "dp", perm)


def over_expert(value, perm):
    return lax.ppermute(value, "expert", perm)


def mm(a, b, dims=((1,), (0,))):
    return lax.dot_general(a, b, (dims, ((), ())), preferred_element_type=F32)


def put(buffer, part, z, row=0):
    return lax.dynamic_update_slice(buffer, part[None], (z, row, 0))


def ring_gather(slab, z, hooks):
    rows = slab.shape[0]
    half = rows // 2
    own = put(jnp.zeros((N_Z,) + slab.shape, slab.dtype), slab, z)
    other = jnp.zeros((N_Z,) + slab.shape, slab.dtype)
    pending = [(slab, z, 0)]

    def swap(other, pending):
        theirs = over_dp(jnp.concatenate([part for part, _, _ in pending], axis=0), PERM_CORE)
        start = 0
        for part, at, row in pending:
            other = put(other, theirs[start : start + part.shape[0]], at, row)
            start = start + part.shape[0]
        return other

    up, down = slab, slab
    for step in range(1, 5):
        if step == 4:
            up, down = up[:half], down[half:]
        if step in hooks:
            up, down = hooks[step](up, down)
        up, down = tie(over_dp(up, PERM_UP), over_dp(down, PERM_DOWN))
        last = half if step == 4 else 0
        pending = pending + [(up, (z - step) % N_Z, 0), (down, (z + step) % N_Z, last)]
        own = put(own, hooks["keep", step](up) if ("keep", step) in hooks else up, (z - step) % N_Z)
        own = put(own, down, (z + step) % N_Z, last)
        if step >= 2:
            other = swap(other, pending)
            pending = []
    return own, other


def ring_scatter(partial_at, z, hooks):
    def at(step):
        return partial_at((z + step) % N_Z)

    def send(up, down):
        return tie(over_dp(up, PERM_UP), over_dp(down, PERM_DOWN))

    far = hooks[1](at(4))
    half = far.shape[0] // 2
    up, down = send(far[:half], far[half:])
    up = hooks[2](up)
    near_up, near_down = at(3), at(5)
    up = jnp.concatenate([near_up[:half] + up, near_up[half:]], axis=0)
    down = jnp.concatenate([near_down[:half], near_down[half:] + down], axis=0)
    up, down = send(up, down)
    up = hooks[3](up)
    up, down = send(at(2) + up, at(-2) + down)
    up = hooks[4](up)
    up, down = send(at(1) + up, at(-1) + down)
    return at(0).astype(F32) + up.astype(F32) + down.astype(F32)


def pack_down(d, ff):
    width = d.shape[-1]
    parts = []
    for lo in range(0, width, ff):
        part = d[..., lo : lo + ff]
        short = ff - part.shape[-1]
        parts.append(jnp.pad(part, [(0, 0)] * (d.ndim - 1) + [(0, short)]) if short else part)
    return jnp.concatenate(parts, axis=-2)


def unpack_down(packed, width):
    rows, ff = packed.shape[-2] // -(-width // packed.shape[-1]), packed.shape[-1]
    parts = [packed[..., k * rows : (k + 1) * rows, : width - k * ff] for k in range(-(-width // ff))]
    return jnp.concatenate(parts, axis=-1)


def pick(first, a, b, axis):
    return jnp.where(first, jnp.concatenate([a, b], axis=axis), jnp.concatenate([b, a], axis=axis))


def swap_blocks(rows, sign):
    n = rows.shape[0] // N_Y
    blocks = [rows[k * n : (k + 1) * n] for k in range(N_Y)]
    one = over_expert(blocks[1], perm_y(sign))
    three = over_expert(blocks[3], perm_y(-sign))
    one, two = tie(one, blocks[2])
    return [blocks[0], one, over_expert(two, perm_y(2)), three]


def tie(*values):
    return lax.optimization_barrier(values)


def slots_of(routes):
    tok_rows = routes.shape[0]
    experts = jnp.arange(EXPERTS, dtype=jnp.int32)
    onehot = (routes[:, :, None] == experts).astype(F32)
    named = jnp.sum(onehot, axis=1).astype(BF)
    earlier = jnp.arange(tok_rows)[:, None] > jnp.arange(tok_rows)[None, :]
    before = mm(earlier.astype(BF), named)
    return jnp.sum(onehot * before[:, None, :], axis=2)


def shards(tokens, routes, route_weights, cotangent, w_gate, w_up, w_down):
    tok_rows, width = tokens.shape
    ff = w_gate.shape[2]
    half_ff = ff // 2
    half_d = width // 2
    dp = lax.axis_index("dp")
    expert = lax.axis_index("expert")
    c, z, x = dp % N_C, (dp // N_C) % N_Z, dp // (N_C * N_Z)
    y, low = expert % N_Y, expert // N_Y
    on_c0, on_x0 = c == 0, x == 0

    wg, wu, wd = w_gate[0], w_up[0], w_down[0]

    def halves(k):
        return jnp.concatenate(
            [
                lax.dynamic_slice_in_dim(wg, k * half_ff, half_ff, 1),
                lax.dynamic_slice_in_dim(wu, k * half_ff, half_ff, 1),
            ],
            axis=1,
        )

    near = pick(on_c0, halves(c), over_dp(halves(1 - c), PERM_CORE), 0)
    down_pair = pick(on_c0, wd, over_dp(wd, PERM_CORE), 0)
    near, down_pair, routes = tie(near, down_pair, routes)
    far = over_dp(near, PERM_X)
    down_slab = jnp.where(x == c, down_pair, over_dp(down_pair, PERM_X_TO))

    packed = jnp.concatenate([routes.astype(F32).T, slots_of(routes).T, route_weights.T], axis=0)
    packed_peer = over_expert(packed, PERM_L)
    token_pair = jnp.concatenate([tokens, cotangent], axis=1)
    tokens_out, packed_peer = tie(tokens, packed_peer)
    tokens_peer = over_expert(tokens_out, PERM_L)

    def tables(info):
        numbers = jnp.arange(N_Y * BLOCK, dtype=jnp.int32)[:, None]
        hits, weights = [], []
        for j in range(2):
            ids = info[j].astype(jnp.int32)
            row = ((ids % N_Y - y) % N_Y) * BLOCK + info[2 + j].astype(jnp.int32)
            row = jnp.where(ids // N_Y == low, row, -1)
            hit = numbers == row[None, :]
            hits.append(hit.astype(F32))
            weights.append(jnp.where(hit, info[4 + j][None, :], 0.0))
        weight = weights[0] + weights[1]
        return (hits[0] + hits[1]).astype(BF), weight, jnp.sum(weight, axis=1, keepdims=True)

    def swapped(values):
        return pick(on_x0, values[:, :half_d], values[:, half_d:], 1)

    def dispatch(table, scale, pair):
        lanes = jnp.concatenate([swapped(pair[:, :width]), pair[:, width:]], axis=1)
        scales = jnp.where(jnp.arange(2 * width) < width, 1.0, scale)
        return swap_blocks((mm(table, lanes) * scales).astype(BF), 1)

    hot, weight, slot_weight = tables(packed)
    hot_peer, weight_peer, slot_weight_peer = tables(packed_peer)

    state = {"got": dispatch(hot, slot_weight, token_pair)}

    def keep_first(part):
        part, *state["got"] = tie(part, *state["got"])
        return part

    def before_second(up, down):
        up, down, state["tokens"], cot_out = tie(up, down, tokens_peer, cotangent)
        state["cot"] = over_expert(cot_out, PERM_L)
        return up, down

    def before_third(up, down):
        up, down, cot_peer = tie(up, down, state["cot"])
        pair = jnp.concatenate([state["tokens"], cot_peer], axis=1)
        state["got_peer"] = dispatch(hot_peer, slot_weight_peer, pair)
        return up, down

    def before_fourth(up, down):
        up, down, *state["got"] = tie(up, down, *state["got"])
        return up, down

    def keep_last(part):
        part, *state["got_peer"] = tie(part, *state["got_peer"])
        return part

    slab = jnp.concatenate([near, far, pack_down(down_slab, ff)], axis=0)
    hooks = {
        2: before_second,
        3: before_third,
        4: before_fourth,
        ("keep", 1): keep_first,
        ("keep", 4): keep_last,
    }
    own, other = ring_gather(slab, z, hooks)
    gu_rows = half_d // N_Z

    def weights(gathered):
        return (
            gathered[:, :gu_rows].reshape(half_d, ff),
            gathered[:, gu_rows : 2 * gu_rows].reshape(half_d, ff),
            unpack_down(gathered[:, 2 * gu_rows :], width).reshape(half_ff, width),
        )

    near_own, far_own, down_own = weights(own)
    near_oth, far_oth, down_oth = weights(other)

    got = jnp.concatenate(state["got"] + state["got_peer"], axis=0)
    rows, grads = got[:, :width], got[:, width:]
    rows_near, rows_far = rows[:, :half_d], rows[:, half_d:]

    def forward(w_near, w_far):
        both_values = mm(rows_near, w_near) + mm(rows_far, w_far)
        gate, up = both_values[:, :half_ff], both_values[:, half_ff:]
        sig = jax.nn.sigmoid(gate)
        return gate, up, sig, (gate * sig * up).astype(BF)

    gate_oth, up_oth, sig_oth, hid_oth = forward(near_oth, far_oth)
    gate_own, up_own, sig_own, hid_own = forward(near_own, far_own)

    def backward(gate, up, sig, w):
        hidden_grad = mm(grads, w, ((1,), (1,)))
        gate_grad = hidden_grad * up * sig * (1.0 + gate * (1.0 - sig))
        up_grad = hidden_grad * gate * sig
        return jnp.concatenate([gate_grad.astype(BF), up_grad.astype(BF)], axis=1)

    def over_rows(a, b):
        return mm(a, b, ((0,), (0,))).astype(BF)

    grad_oth = backward(gate_oth, up_oth, sig_oth, down_oth)
    grad_own = backward(gate_own, up_own, sig_own, down_own)

    def both_cores(left, own_half, other_half, rows_z):
        theirs = over_dp(over_rows(left[1], other_half), PERM_CORE)
        summed = over_rows(left[0], own_half) + theirs
        return summed.reshape(N_Z, rows_z, summed.shape[1])

    part_near = both_cores((rows_near, rows_near), grad_own, grad_oth, gu_rows)
    part_far = both_cores((rows_far, rows_far), grad_own, grad_oth, gu_rows)
    part_down = both_cores((hid_own, hid_oth), grads, grads, half_ff // N_Z)

    def partial_at(k):
        near_k, far_k, down_k = (
            lax.dynamic_index_in_dim(part, k, 0, keepdims=False)
            for part in (part_near, part_far, part_down)
        )
        return jnp.concatenate([near_k, far_k, pack_down(down_k, ff)], axis=0)

    def input_grad(own, oth):
        return (mm(grad_own, own, ((1,), (1,))) + mm(grad_oth, oth, ((1,), (1,)))).astype(BF)

    def weighted(weight, values):
        high = weight.astype(BF)
        rest = (weight - high.astype(F32)).astype(BF)
        return mm(high, values, ((0,), (0,))) + mm(rest, values, ((0,), (0,)))

    def summed(hot, values):
        return mm(hot, values, ((0,), (0,)))

    def before_first(value):
        nonlocal grad_own, grad_oth
        value, hid_1, hid_2, grad_own, grad_oth = tie(value, hid_own, hid_oth, grad_own, grad_oth)
        output = (mm(hid_1, down_own) + mm(hid_2, down_oth)).astype(BF)
        inputs = [input_grad(near_own, near_oth), input_grad(far_own, far_oth)]
        results = jnp.concatenate([output, *inputs], axis=1)
        split = N_Y * BLOCK
        *got, home = tie(*swap_blocks(results[split:], -1), results[:split])
        state["back_peer"] = jnp.concatenate(got, axis=0)
        state["back"] = jnp.concatenate(swap_blocks(home, -1), axis=0)
        return value

    def before_third(value):
        value, late_weight, state["hot_peer"] = tie(value, weight_peer, hot_peer)
        mixed = weighted(late_weight, state["back_peer"][:, :width]).astype(BF)
        state["mixed_peer"] = over_expert(mixed, PERM_L)
        return value

    def before_fourth(value):
        sums = summed(state["hot_peer"], state["back_peer"][:, width:]).astype(BF)
        value, state["mixed_peer"], sums = tie(value, state["mixed_peer"], sums)
        state["sums_peer"] = over_expert(sums, PERM_L)
        value, state["hot"], state["weight"] = tie(value, hot, weight)
        return value

    hooks = {1: before_first, 2: lambda value: value, 3: before_third, 4: before_fourth}
    total = ring_scatter(partial_at, z, hooks)
    back = state["back"]
    mixed = weighted(state["weight"], back[:, :width]) + state["mixed_peer"].astype(F32)
    mixed = mixed.astype(BF)

    gu_part, down_part = gu_rows // 2, 3 * wd.shape[0]

    def rows_of(k):
        near_rows = lax.dynamic_slice_in_dim(total[: 2 * gu_part], k * gu_part, gu_part, 0)
        far_rows = lax.dynamic_slice_in_dim(total[2 * gu_part : 4 * gu_part], k * gu_part, gu_part, 0)
        down = total[4 * gu_part :].reshape(3, 2 * down_part // 3, ff)
        down = lax.dynamic_slice_in_dim(down, k * (down_part // 3), down_part // 3, 1)
        return near_rows, far_rows, down.reshape(down_part, ff)

    near_keep, far_keep, down_keep = rows_of(c)
    took = over_dp(jnp.concatenate(rows_of(1 - c), axis=0).astype(BF), PERM_CORE)
    near_took, far_took, down_took = jnp.split(took, [gu_part, 2 * gu_part], axis=0)
    down_took = down_took.astype(F32)
    down_mine = jnp.where(x == c, down_keep, down_took)
    down_give = jnp.where(x == c, down_took, down_keep).astype(BF)
    give = jnp.concatenate([far_keep.astype(BF), far_took, down_give], axis=0)
    give, sums_peer = tie(give, state["sums_peer"])
    got = over_dp(give, PERM_X).astype(F32)
    near_keep = (near_keep + got[:gu_part]).astype(BF)
    near_took = (near_took.astype(F32) + got[gu_part : 2 * gu_part]).astype(BF)
    grad_gate = pick(on_c0, near_keep[:, :half_ff], near_took[:, :half_ff], 1)
    grad_up = pick(on_c0, near_keep[:, half_ff:], near_took[:, half_ff:], 1)
    grad_down = unpack_down((down_mine + got[2 * gu_part :]).astype(BF), width)

    token_grad = summed(state["hot"], back[:, width:]) + sums_peer.astype(F32)
    token_grad = swapped(token_grad.astype(BF))

    return mixed, token_grad, grad_gate[None], grad_up[None], grad_down[None]


def solution(mesh):
    in_specs = (
        P(("dp", "expert"), None),
        P(("dp", "expert"), None),
        P(("dp", "expert"), None),
        P(("dp", "expert"), None),
        P("expert", "dp", None),
        P("expert", "dp", None),
        P("expert", "dp", None),
    )
    out_specs = (
        P(("dp", "expert"), None),
        P(("dp", "expert"), None),
        P("expert", "dp", None),
        P("expert", "dp", None),
        P("expert", "dp", None),
    )
    return jax.shard_map(shards, mesh=mesh, in_specs=in_specs, out_specs=out_specs, check_vma=False)
```

```python
import jax
import jax.numpy as jnp
from jax import lax
from jax.sharding import PartitionSpec as P

EXPERTS = 8
BLOCK = 64
N_X, N_Z, N_C = 2, 8, 2
N_L, N_Y = 2, 4
BF = jnp.bfloat16
F32 = jnp.float32


def dp_index(x, z, c):
    return (x * N_Z + z) * N_C + c


DP_ALL = [(x, z, c) for x in range(N_X) for z in range(N_Z) for c in range(N_C)]
PERM_UP = [(dp_index(x, z, c), dp_index(x, (z + 1) % N_Z, c)) for x, z, c in DP_ALL]
PERM_DOWN = [(dp_index(x, z, c), dp_index(x, (z - 1) % N_Z, c)) for x, z, c in DP_ALL]
PERM_CORE = [(dp_index(x, z, c), dp_index(x, z, 1 - c)) for x, z, c in DP_ALL]
PERM_X = [(dp_index(x, z, c), dp_index(1 - x, z, c)) for x, z, c in DP_ALL]
PERM_X_TO = [(dp_index(c, z, c), dp_index(1 - c, z, c)) for z in range(N_Z) for c in range(N_C)]
PERM_L = [(a * N_Y + y, (1 - a) * N_Y + y) for a in range(N_L) for y in range(N_Y)]


def perm_y(shift):
    return [(a * N_Y + y, a * N_Y + (y + shift) % N_Y) for a in range(N_L) for y in range(N_Y)]


def over_dp(value, perm):
    return lax.ppermute(value, "dp", perm)


def over_expert(value, perm):
    return lax.ppermute(value, "expert", perm)


def mm(a, b, dims=((1,), (0,))):
    return lax.dot_general(a, b, (dims, ((), ())), preferred_element_type=F32)


def put(buffer, part, z, row=0):
    return lax.dynamic_update_slice(buffer, part[None], (z, row, 0))


def ring_gather(slab, z, hooks):
    rows = slab.shape[0]
    half = rows // 2
    own = put(jnp.zeros((N_Z,) + slab.shape, slab.dtype), slab, z)
    up, down = slab, slab
    for step in range(1, 5):
        if step == 4:
            up, down = up[:half], down[half:]
        if step in hooks:
            up, down = hooks[step](up, down)
        up, down = tie(over_dp(up, PERM_UP), over_dp(down, PERM_DOWN))
        if step == 4:
            up, down = hooks[5](up, down)
        last = half if step == 4 else 0
        own = put(own, hooks["keep", step](up) if ("keep", step) in hooks else up, (z - step) % N_Z)
        own = put(own, down, (z + step) % N_Z, last)
    return own, over_dp(own, PERM_CORE)


def ring_scatter(partial_at, z, hooks):
    def at(step):
        return partial_at((z + step) % N_Z)

    def send(up, down):
        return tie(over_dp(up, PERM_UP), over_dp(down, PERM_DOWN))

    far = hooks[1](at(4))
    half = far.shape[0] // 2
    up, down = send(far[:half], far[half:])
    up = hooks[2](up)
    near_up, near_down = at(3), at(5)
    up = jnp.concatenate([near_up[:half] + up, near_up[half:]], axis=0)
    down = jnp.concatenate([near_down[:half], near_down[half:] + down], axis=0)
    up, down = send(up, down)
    up = hooks[3](up)
    up, down = send(at(2) + up, at(-2) + down)
    up = hooks[4](up)
    up, down = send(at(1) + up, at(-1) + down)
    return at(0).astype(F32) + up.astype(F32) + down.astype(F32)


def pack_down(d, ff):
    width = d.shape[-1]
    parts = []
    for lo in range(0, width, ff):
        part = d[..., lo : lo + ff]
        short = ff - part.shape[-1]
        parts.append(jnp.pad(part, [(0, 0)] * (d.ndim - 1) + [(0, short)]) if short else part)
    return jnp.concatenate(parts, axis=-2)


def unpack_down(packed, width):
    rows, ff = packed.shape[-2] // -(-width // packed.shape[-1]), packed.shape[-1]
    parts = [packed[..., k * rows : (k + 1) * rows, : width - k * ff] for k in range(-(-width // ff))]
    return jnp.concatenate(parts, axis=-1)


def pick(first, a, b, axis):
    return jnp.where(first, jnp.concatenate([a, b], axis=axis), jnp.concatenate([b, a], axis=axis))


def four_blocks(rows):
    n = rows.shape[0] // N_Y
    return [rows[k * n : (k + 1) * n] for k in range(N_Y)]


def swap_near(blocks, sign):
    return over_expert(blocks[1], perm_y(sign)), over_expert(blocks[3], perm_y(-sign))


def swap_blocks(rows, sign, at_once):
    blocks = four_blocks(rows)
    one, three = swap_near(blocks, sign)
    two = blocks[2]
    if not at_once:
        one, two = tie(one, two)
    return [blocks[0], one, over_expert(two, perm_y(2)), three]


def tie(*values):
    return lax.optimization_barrier(values)


def slots_of(routes):
    tok_rows = routes.shape[0]
    experts = jnp.arange(EXPERTS, dtype=jnp.int32)
    onehot = (routes[:, :, None] == experts).astype(F32)
    named = jnp.sum(onehot, axis=1).astype(BF)
    earlier = jnp.arange(tok_rows)[:, None] > jnp.arange(tok_rows)[None, :]
    before = mm(earlier.astype(BF), named)
    return jnp.sum(onehot * before[:, None, :], axis=2)


def shards(tokens, routes, route_weights, cotangent, w_gate, w_up, w_down):
    tok_rows, width = tokens.shape
    ff = w_gate.shape[2]
    half_ff = ff // 2
    half_d = width // 2
    dp = lax.axis_index("dp")
    expert = lax.axis_index("expert")
    c, z, x = dp % N_C, (dp // N_C) % N_Z, dp // (N_C * N_Z)
    y, low = expert % N_Y, expert // N_Y
    on_c0, on_x0 = c == 0, x == 0

    wg, wu, wd = w_gate[0], w_up[0], w_down[0]

    def halves(k):
        return jnp.concatenate(
            [
                lax.dynamic_slice_in_dim(wg, k * half_ff, half_ff, 1),
                lax.dynamic_slice_in_dim(wu, k * half_ff, half_ff, 1),
            ],
            axis=1,
        )

    near = pick(on_c0, halves(c), over_dp(halves(1 - c), PERM_CORE), 0)
    down_pair = pick(on_c0, wd, over_dp(wd, PERM_CORE), 0)
    near, down_pair, routes = tie(near, down_pair, routes)
    far = over_dp(near, PERM_X)
    down_slab = jnp.where(x == c, down_pair, over_dp(down_pair, PERM_X_TO))

    packed = jnp.concatenate([routes.astype(F32).T, slots_of(routes).T, route_weights.T], axis=0)
    packed_peer = over_expert(packed, PERM_L)
    token_pair = jnp.concatenate([tokens, cotangent], axis=1)
    tokens_out, packed_peer = tie(tokens, packed_peer)
    tokens_peer = over_expert(tokens_out, PERM_L)

    def tables(info):
        numbers = jnp.arange(N_Y * BLOCK, dtype=jnp.int32)[:, None]
        hits, weights = [], []
        for j in range(2):
            ids = info[j].astype(jnp.int32)
            row = ((ids % N_Y - y) % N_Y) * BLOCK + info[2 + j].astype(jnp.int32)
            row = jnp.where(ids // N_Y == low, row, -1)
            hit = numbers == row[None, :]
            hits.append(hit.astype(F32))
            weights.append(jnp.where(hit, info[4 + j][None, :], 0.0))
        weight = weights[0] + weights[1]
        return (hits[0] + hits[1]).astype(BF), weight, jnp.sum(weight, axis=1, keepdims=True)

    def swapped(values):
        return pick(on_x0, values[:, :half_d], values[:, half_d:], 1)

    def dispatch(table, scale, pair, at_once):
        lanes = jnp.concatenate([swapped(pair[:, :width]), pair[:, width:]], axis=1)
        scales = jnp.where(jnp.arange(2 * width) < width, 1.0, scale)
        return swap_blocks((mm(table, lanes) * scales).astype(BF), 1, at_once)

    hot, weight, slot_weight = tables(packed)
    hot_peer, weight_peer, slot_weight_peer = tables(packed_peer)

    state = {"got": dispatch(hot, slot_weight, token_pair, False)}

    def keep_first(part):
        part, *state["got"] = tie(part, *state["got"])
        return part

    def before_second(up, down):
        up, down, tokens_in, cot_out = tie(up, down, tokens_peer, cotangent)
        state["cot"] = over_expert(cot_out, PERM_L)
        sent = mm(hot_peer, swapped(tokens_in)).astype(BF)
        *state["got"], sent = tie(*state["got"], sent)
        state["rows"] = four_blocks(sent)
        state["rows_near"] = swap_near(state["rows"], 1)
        return up, down

    def before_third(up, down):
        up, down, *state["rows_near"] = tie(up, down, *state["rows_near"])
        grads = four_blocks((mm(hot_peer, state["cot"]) * slot_weight_peer).astype(BF))
        state["two"] = over_expert(jnp.concatenate([state["rows"][2], grads[2]], axis=1), perm_y(2))
        state["grads_near"] = swap_near(grads, 1)
        state["grads"] = grads
        return up, down

    def after_fourth(up, down):
        up, down, state["two"], *state["grads_near"] = tie(up, down, state["two"], *state["grads_near"])
        return up, down

    slab = jnp.concatenate([near, far, pack_down(down_slab, ff)], axis=0)
    hooks = {
        2: before_second,
        3: before_third,
        5: after_fourth,
        ("keep", 1): keep_first,
    }
    own, other = ring_gather(slab, z, hooks)
    gu_rows = half_d // N_Z

    def weights(gathered):
        return (
            gathered[:, :gu_rows].reshape(half_d, ff),
            gathered[:, gu_rows : 2 * gu_rows].reshape(half_d, ff),
            unpack_down(gathered[:, 2 * gu_rows :], width).reshape(half_ff, width),
        )

    near_own, far_own, down_own = weights(own)
    near_oth, far_oth, down_oth = weights(other)

    (grads_one, grads_three), (rows_one, rows_three) = state["grads_near"], state["rows_near"]
    peer = [(state["rows"][0], state["grads"][0]), (rows_one, grads_one), (rows_three, grads_three)]
    peer = [jnp.concatenate(block, axis=1) for block in peer]
    got = jnp.concatenate([*state["got"], *peer[:2], state["two"], peer[2]], axis=0)
    rows, grads = got[:, :width], got[:, width:]
    rows_near, rows_far = rows[:, :half_d], rows[:, half_d:]

    def forward(w_near, w_far):
        both_values = mm(rows_near, w_near) + mm(rows_far, w_far)
        gate, up = both_values[:, :half_ff], both_values[:, half_ff:]
        sig = jax.nn.sigmoid(gate)
        return gate, up, sig, (gate * sig * up).astype(BF)

    gate_oth, up_oth, sig_oth, hid_oth = forward(near_oth, far_oth)
    gate_own, up_own, sig_own, hid_own = forward(near_own, far_own)

    def backward(gate, up, sig, w):
        hidden_grad = mm(grads, w, ((1,), (1,)))
        gate_grad = hidden_grad * up * sig * (1.0 + gate * (1.0 - sig))
        up_grad = hidden_grad * gate * sig
        return jnp.concatenate([gate_grad.astype(BF), up_grad.astype(BF)], axis=1)

    def over_rows(a, b):
        return mm(a, b, ((0,), (0,))).astype(BF)

    grad_oth = backward(gate_oth, up_oth, sig_oth, down_oth)
    grad_own = backward(gate_own, up_own, sig_own, down_own)

    def both_cores(left, own_half, other_half, rows_z):
        theirs = over_dp(over_rows(left[1], other_half), PERM_CORE)
        summed = over_rows(left[0], own_half) + theirs
        return summed.reshape(N_Z, rows_z, summed.shape[1])

    part_near = both_cores((rows_near, rows_near), grad_own, grad_oth, gu_rows)
    part_far = both_cores((rows_far, rows_far), grad_own, grad_oth, gu_rows)
    part_down = both_cores((hid_own, hid_oth), grads, grads, half_ff // N_Z)

    def partial_at(k):
        near_k, far_k, down_k = (
            lax.dynamic_index_in_dim(part, k, 0, keepdims=False)
            for part in (part_near, part_far, part_down)
        )
        return jnp.concatenate([near_k, far_k, pack_down(down_k, ff)], axis=0)

    def input_grad(own, oth):
        return (mm(grad_own, own, ((1,), (1,))) + mm(grad_oth, oth, ((1,), (1,)))).astype(BF)

    def weighted(weight, values):
        high = weight.astype(BF)
        rest = (weight - high.astype(F32)).astype(BF)
        return mm(high, values, ((0,), (0,))) + mm(rest, values, ((0,), (0,)))

    def summed(hot, values):
        return mm(hot, values, ((0,), (0,)))

    def before_first(value):
        output = (mm(hid_own, down_own) + mm(hid_oth, down_oth)).astype(BF)
        inputs = [input_grad(near_own, near_oth), input_grad(far_own, far_oth)]
        value, results = tie(value, jnp.concatenate([output, *inputs], axis=1))
        split = N_Y * BLOCK
        *got, home = tie(*swap_blocks(results[split:], -1, False), results[:split])
        state["back_peer"] = jnp.concatenate(got, axis=0)
        state["back"] = jnp.concatenate(swap_blocks(home, -1, False), axis=0)
        return value

    def before_third(value):
        value, late_weight, state["hot_peer"] = tie(value, weight_peer, hot_peer)
        mixed = weighted(late_weight, state["back_peer"][:, :width]).astype(BF)
        state["mixed_peer"] = over_expert(mixed, PERM_L)
        return value

    def before_fourth(value):
        sums = summed(state["hot_peer"], state["back_peer"][:, width:]).astype(BF)
        value, state["mixed_peer"], sums = tie(value, state["mixed_peer"], sums)
        state["sums_peer"] = over_expert(sums, PERM_L)
        value, state["hot"], state["weight"] = tie(value, hot, weight)
        return value

    hooks = {1: before_first, 2: lambda value: value, 3: before_third, 4: before_fourth}
    total = ring_scatter(partial_at, z, hooks)
    back = state["back"]
    mixed = weighted(state["weight"], back[:, :width]) + state["mixed_peer"].astype(F32)
    mixed = mixed.astype(BF)

    gu_part, down_part = gu_rows // 2, 3 * wd.shape[0]

    def rows_of(k):
        near_rows = lax.dynamic_slice_in_dim(total[: 2 * gu_part], k * gu_part, gu_part, 0)
        far_rows = lax.dynamic_slice_in_dim(total[2 * gu_part : 4 * gu_part], k * gu_part, gu_part, 0)
        down = total[4 * gu_part :].reshape(3, 2 * down_part // 3, ff)
        down = lax.dynamic_slice_in_dim(down, k * (down_part // 3), down_part // 3, 1)
        return near_rows, far_rows, down.reshape(down_part, ff)

    near_keep, far_keep, down_keep = rows_of(c)
    took = over_dp(jnp.concatenate(rows_of(1 - c), axis=0).astype(BF), PERM_CORE)
    near_took, far_took, down_took = jnp.split(took, [gu_part, 2 * gu_part], axis=0)
    down_took = down_took.astype(F32)
    down_mine = jnp.where(x == c, down_keep, down_took)
    down_give = jnp.where(x == c, down_took, down_keep).astype(BF)
    give = jnp.concatenate([far_keep.astype(BF), far_took, down_give], axis=0)
    give, sums_peer = tie(give, state["sums_peer"])
    got = over_dp(give, PERM_X).astype(F32)
    near_keep = (near_keep + got[:gu_part]).astype(BF)
    near_took = (near_took.astype(F32) + got[gu_part : 2 * gu_part]).astype(BF)
    grad_gate = pick(on_c0, near_keep[:, :half_ff], near_took[:, :half_ff], 1)
    grad_up = pick(on_c0, near_keep[:, half_ff:], near_took[:, half_ff:], 1)
    grad_down = unpack_down((down_mine + got[2 * gu_part :]).astype(BF), width)

    token_grad = summed(state["hot"], back[:, width:]) + sums_peer.astype(F32)
    token_grad = swapped(token_grad.astype(BF))

    return mixed, token_grad, grad_gate[None], grad_up[None], grad_down[None]


def solution(mesh):
    in_specs = (
        P(("dp", "expert"), None),
        P(("dp", "expert"), None),
        P(("dp", "expert"), None),
        P(("dp", "expert"), None),
        P("expert", "dp", None),
        P("expert", "dp", None),
        P("expert", "dp", None),
    )
    out_specs = (
        P(("dp", "expert"), None),
        P(("dp", "expert"), None),
        P("expert", "dp", None),
        P("expert", "dp", None),
        P("expert", "dp", None),
    )
    return jax.shard_map(shards, mesh=mesh, in_specs=in_specs, out_specs=out_specs, check_vma=False)
```

```python
import jax
import jax.numpy as jnp
from jax import lax
from jax.sharding import PartitionSpec as P

EXPERTS = 8
BLOCK = 64
N_X, N_Z, N_C = 2, 8, 2
N_L, N_Y = 2, 4
BF = jnp.bfloat16
F32 = jnp.float32


def dp_index(x, z, c):
    return (x * N_Z + z) * N_C + c


DP_ALL = [(x, z, c) for x in range(N_X) for z in range(N_Z) for c in range(N_C)]
PERM_UP = [(dp_index(x, z, c), dp_index(x, (z + 1) % N_Z, c)) for x, z, c in DP_ALL]
PERM_DOWN = [(dp_index(x, z, c), dp_index(x, (z - 1) % N_Z, c)) for x, z, c in DP_ALL]
PERM_CORE = [(dp_index(x, z, c), dp_index(x, z, 1 - c)) for x, z, c in DP_ALL]
PERM_X = [(dp_index(x, z, c), dp_index(1 - x, z, c)) for x, z, c in DP_ALL]
PERM_X_TO = [(dp_index(c, z, c), dp_index(1 - c, z, c)) for z in range(N_Z) for c in range(N_C)]
PERM_L = [(a * N_Y + y, (1 - a) * N_Y + y) for a in range(N_L) for y in range(N_Y)]


def perm_y(shift):
    return [(a * N_Y + y, a * N_Y + (y + shift) % N_Y) for a in range(N_L) for y in range(N_Y)]


def over_dp(value, perm):
    return lax.ppermute(value, "dp", perm)


def over_expert(value, perm):
    return lax.ppermute(value, "expert", perm)


def mm(a, b, dims=((1,), (0,))):
    return lax.dot_general(a, b, (dims, ((), ())), preferred_element_type=F32)


def put(buffer, part, z, row=0):
    return lax.dynamic_update_slice(buffer, part[None], (z, row, 0))


def ring_gather(slab, z, hooks):
    rows = slab.shape[0]
    half = rows // 2
    own = put(jnp.zeros((N_Z,) + slab.shape, slab.dtype), slab, z)
    up, down = slab, slab
    for step in range(1, 5):
        if step == 4:
            up, down = up[:half], down[half:]
        if step in hooks:
            up, down = hooks[step](up, down)
        up, down = tie(over_dp(up, PERM_UP), over_dp(down, PERM_DOWN))
        if step == 4:
            up, down = hooks[5](up, down)
        last = half if step == 4 else 0
        own = put(own, hooks["keep", step](up) if ("keep", step) in hooks else up, (z - step) % N_Z)
        own = put(own, down, (z + step) % N_Z, last)
    return own, over_dp(own, PERM_CORE)


def ring_scatter(partial_at, z, hooks):
    def at(step):
        return partial_at((z + step) % N_Z)

    def send(up, down):
        return tie(over_dp(up, PERM_UP), over_dp(down, PERM_DOWN))

    far = hooks[1](at(4))
    half = far.shape[0] // 2
    up, down = send(far[:half], far[half:])
    up = hooks[2](up)
    near_up, near_down = at(3), at(5)
    up = jnp.concatenate([near_up[:half] + up, near_up[half:]], axis=0)
    down = jnp.concatenate([near_down[:half], near_down[half:] + down], axis=0)
    up, down = send(up, down)
    up = hooks[3](up)
    up, down = send(at(2) + up, at(-2) + down)
    up = hooks[4](up)
    up, down = send(at(1) + up, at(-1) + down)
    return at(0).astype(F32) + up.astype(F32) + down.astype(F32)


def pack_down(d, ff):
    group = d.shape[-2] // 3
    last = [d[..., k * group : (k + 1) * group, 2 * ff :] for k in range(3)]
    last = jnp.concatenate(last, axis=-1)
    parts = [d[..., :ff], d[..., ff : 2 * ff], last[..., :ff], last[..., ff:]]
    return jnp.concatenate(parts, axis=-2)


def unpack_down(packed, width):
    ff = packed.shape[-1]
    group = packed.shape[-2] // 8
    short = width - 2 * ff
    last = jnp.concatenate([packed[..., 6 * group : 7 * group, :], packed[..., 7 * group :, :]], axis=-1)
    last = [last[..., k * short : (k + 1) * short] for k in range(3)]
    parts = [packed[..., : 3 * group, :], packed[..., 3 * group : 6 * group, :], jnp.concatenate(last, axis=-2)]
    return jnp.concatenate(parts, axis=-1)


def pick(first, a, b, axis):
    return jnp.where(first, jnp.concatenate([a, b], axis=axis), jnp.concatenate([b, a], axis=axis))


def four_blocks(rows):
    n = rows.shape[0] // N_Y
    return [rows[k * n : (k + 1) * n] for k in range(N_Y)]


def swap_near(blocks, sign):
    return over_expert(blocks[1], perm_y(sign)), over_expert(blocks[3], perm_y(-sign))


def swap_blocks(rows, sign, at_once):
    blocks = four_blocks(rows)
    one, three = swap_near(blocks, sign)
    two = blocks[2]
    if not at_once:
        one, two = tie(one, two)
    return [blocks[0], one, over_expert(two, perm_y(2)), three]


def tie(*values):
    return lax.optimization_barrier(values)


def slots_of(routes):
    tok_rows = routes.shape[0]
    experts = jnp.arange(EXPERTS, dtype=jnp.int32)
    onehot = (routes[:, :, None] == experts).astype(F32)
    named = jnp.sum(onehot, axis=1).astype(BF)
    earlier = jnp.arange(tok_rows)[:, None] > jnp.arange(tok_rows)[None, :]
    before = mm(earlier.astype(BF), named)
    return jnp.sum(onehot * before[:, None, :], axis=2)


def shards(tokens, routes, route_weights, cotangent, w_gate, w_up, w_down):
    tok_rows, width = tokens.shape
    ff = w_gate.shape[2]
    half_ff = ff // 2
    half_d = width // 2
    dp = lax.axis_index("dp")
    expert = lax.axis_index("expert")
    c, z, x = dp % N_C, (dp // N_C) % N_Z, dp // (N_C * N_Z)
    y, low = expert % N_Y, expert // N_Y
    on_c0, on_x0 = c == 0, x == 0

    wg, wu, wd = w_gate[0], w_up[0], w_down[0]

    def halves(k):
        return jnp.concatenate(
            [
                lax.dynamic_slice_in_dim(wg, k * half_ff, half_ff, 1),
                lax.dynamic_slice_in_dim(wu, k * half_ff, half_ff, 1),
            ],
            axis=1,
        )

    near = pick(on_c0, halves(c), over_dp(halves(1 - c), PERM_CORE), 0)
    down_pair = pick(on_c0, wd, over_dp(wd, PERM_CORE), 0)
    near, down_pair, routes = tie(near, down_pair, routes)
    far = over_dp(near, PERM_X)
    down_slab = jnp.where(x == c, down_pair, over_dp(down_pair, PERM_X_TO))

    packed = jnp.concatenate([routes.astype(F32).T, slots_of(routes).T, route_weights.T], axis=0)
    packed_peer = over_expert(packed, PERM_L)
    token_pair = jnp.concatenate([tokens, cotangent], axis=1)
    tokens_out, packed_peer = tie(tokens, packed_peer)
    tokens_peer = over_expert(tokens_out, PERM_L)

    def tables(info):
        numbers = jnp.arange(N_Y * BLOCK, dtype=jnp.int32)[:, None]
        hits, weights = [], []
        for j in range(2):
            ids = info[j].astype(jnp.int32)
            row = ((ids % N_Y - y) % N_Y) * BLOCK + info[2 + j].astype(jnp.int32)
            row = jnp.where(ids // N_Y == low, row, -1)
            hit = numbers == row[None, :]
            hits.append(hit.astype(F32))
            weights.append(jnp.where(hit, info[4 + j][None, :], 0.0))
        weight = weights[0] + weights[1]
        return (hits[0] + hits[1]).astype(BF), weight, jnp.sum(weight, axis=1, keepdims=True)

    def swapped(values):
        return pick(on_x0, values[:, :half_d], values[:, half_d:], 1)

    def dispatch(table, scale, pair, at_once):
        lanes = jnp.concatenate([swapped(pair[:, :width]), pair[:, width:]], axis=1)
        scales = jnp.where(jnp.arange(2 * width) < width, 1.0, scale)
        return swap_blocks((mm(table, lanes) * scales).astype(BF), 1, at_once)

    hot, weight, slot_weight = tables(packed)
    hot_peer, weight_peer, slot_weight_peer = tables(packed_peer)

    state = {"got": dispatch(hot, slot_weight, token_pair, False)}

    def keep_first(part):
        part, *state["got"] = tie(part, *state["got"])
        return part

    def before_second(up, down):
        up, down, tokens_in, cot_out = tie(up, down, tokens_peer, cotangent)
        state["cot"] = over_expert(cot_out, PERM_L)
        sent = mm(hot_peer, swapped(tokens_in)).astype(BF)
        *state["got"], sent = tie(*state["got"], sent)
        state["rows"] = four_blocks(sent)
        state["rows_near"] = swap_near(state["rows"], 1)
        return up, down

    def before_third(up, down):
        up, down, *state["rows_near"] = tie(up, down, *state["rows_near"])
        grads = four_blocks((mm(hot_peer, state["cot"]) * slot_weight_peer).astype(BF))
        state["two"] = over_expert(jnp.concatenate([state["rows"][2], grads[2]], axis=1), perm_y(2))
        state["grads_near"] = swap_near(grads, 1)
        state["grads"] = grads
        return up, down

    def after_fourth(up, down):
        up, down, state["two"], *state["grads_near"] = tie(up, down, state["two"], *state["grads_near"])
        return up, down

    slab = jnp.concatenate([near, far, pack_down(down_slab, ff)], axis=0)
    hooks = {
        2: before_second,
        3: before_third,
        5: after_fourth,
        ("keep", 1): keep_first,
    }
    own, other = ring_gather(slab, z, hooks)
    gu_rows = half_d // N_Z

    def weights(gathered):
        return (
            gathered[:, :gu_rows].reshape(half_d, ff),
            gathered[:, gu_rows : 2 * gu_rows].reshape(half_d, ff),
            unpack_down(gathered[:, 2 * gu_rows :], width).reshape(half_ff, width),
        )

    near_own, far_own, down_own = weights(own)
    near_oth, far_oth, down_oth = weights(other)

    (grads_one, grads_three), (rows_one, rows_three) = state["grads_near"], state["rows_near"]
    peer = [(state["rows"][0], state["grads"][0]), (rows_one, grads_one), (rows_three, grads_three)]
    peer = [jnp.concatenate(block, axis=1) for block in peer]
    got = jnp.concatenate([*state["got"], *peer[:2], state["two"], peer[2]], axis=0)
    rows, grads = got[:, :width], got[:, width:]
    rows_near, rows_far = rows[:, :half_d], rows[:, half_d:]

    def forward(w_near, w_far):
        both_values = mm(rows_near, w_near) + mm(rows_far, w_far)
        gate, up = both_values[:, :half_ff], both_values[:, half_ff:]
        sig = jax.nn.sigmoid(gate)
        return gate, up, sig, (gate * sig * up).astype(BF)

    gate_oth, up_oth, sig_oth, hid_oth = forward(near_oth, far_oth)
    gate_own, up_own, sig_own, hid_own = forward(near_own, far_own)

    def backward(gate, up, sig, w):
        hidden_grad = mm(grads, w, ((1,), (1,)))
        gate_grad = hidden_grad * up * sig * (1.0 + gate * (1.0 - sig))
        up_grad = hidden_grad * gate * sig
        return jnp.concatenate([gate_grad.astype(BF), up_grad.astype(BF)], axis=1)

    def over_rows(a, b):
        return mm(a, b, ((0,), (0,))).astype(BF)

    grad_oth = backward(gate_oth, up_oth, sig_oth, down_oth)
    grad_own = backward(gate_own, up_own, sig_own, down_own)

    def both_cores(left, own_half, other_half, rows_z):
        theirs = over_dp(over_rows(left[1], other_half), PERM_CORE)
        summed = over_rows(left[0], own_half) + theirs
        return summed.reshape(N_Z, rows_z, summed.shape[1])

    part_near = both_cores((rows_near, rows_near), grad_own, grad_oth, gu_rows)
    part_far = both_cores((rows_far, rows_far), grad_own, grad_oth, gu_rows)
    part_down = both_cores((hid_own, hid_oth), grads, grads, half_ff // N_Z)

    def partial_at(k):
        near_k, far_k, down_k = (
            lax.dynamic_index_in_dim(part, k, 0, keepdims=False)
            for part in (part_near, part_far, part_down)
        )
        return jnp.concatenate([near_k, far_k, pack_down(down_k, ff)], axis=0)

    def input_grad(own, oth):
        return (mm(grad_own, own, ((1,), (1,))) + mm(grad_oth, oth, ((1,), (1,)))).astype(BF)

    def weighted(weight, values):
        high = weight.astype(BF)
        rest = (weight - high.astype(F32)).astype(BF)
        return mm(high, values, ((0,), (0,))) + mm(rest, values, ((0,), (0,)))

    def summed(hot, values):
        return mm(hot, values, ((0,), (0,)))

    def before_first(value):
        output = (mm(hid_own, down_own) + mm(hid_oth, down_oth)).astype(BF)
        inputs = [input_grad(near_own, near_oth), input_grad(far_own, far_oth)]
        value, results = tie(value, jnp.concatenate([output, *inputs], axis=1))
        split = N_Y * BLOCK
        *got, home = tie(*swap_blocks(results[split:], -1, False), results[:split])
        state["back_peer"] = jnp.concatenate(got, axis=0)
        state["back"] = jnp.concatenate(swap_blocks(home, -1, False), axis=0)
        return value

    def before_third(value):
        value, late_weight, state["hot_peer"] = tie(value, weight_peer, hot_peer)
        mixed = weighted(late_weight, state["back_peer"][:, :width]).astype(BF)
        state["mixed_peer"] = over_expert(mixed, PERM_L)
        return value

    def before_fourth(value):
        sums = summed(state["hot_peer"], state["back_peer"][:, width:]).astype(BF)
        value, state["mixed_peer"], sums = tie(value, state["mixed_peer"], sums)
        state["sums_peer"] = over_expert(sums, PERM_L)
        value, state["hot"], state["weight"] = tie(value, hot, weight)
        return value

    hooks = {1: before_first, 2: lambda value: value, 3: before_third, 4: before_fourth}
    total = ring_scatter(partial_at, z, hooks)
    back = state["back"]
    mixed = weighted(state["weight"], back[:, :width]) + state["mixed_peer"].astype(F32)
    mixed = mixed.astype(BF)

    gu_part, down_part = gu_rows // 2, wd.shape[0]

    sum_down = unpack_down(total[4 * gu_part :], width)

    def rows_of(k):
        near_rows = lax.dynamic_slice_in_dim(total[: 2 * gu_part], k * gu_part, gu_part, 0)
        far_rows = lax.dynamic_slice_in_dim(total[2 * gu_part : 4 * gu_part], k * gu_part, gu_part, 0)
        down = lax.dynamic_slice_in_dim(sum_down, k * down_part, down_part, 0)
        return near_rows, far_rows, pack_down(down, ff)

    near_keep, far_keep, down_keep = rows_of(c)
    took = over_dp(jnp.concatenate(rows_of(1 - c), axis=0).astype(BF), PERM_CORE)
    near_took, far_took, down_took = jnp.split(took, [gu_part, 2 * gu_part], axis=0)
    down_took = down_took.astype(F32)
    down_mine = jnp.where(x == c, down_keep, down_took)
    down_give = jnp.where(x == c, down_took, down_keep).astype(BF)
    give = jnp.concatenate([far_keep.astype(BF), far_took, down_give], axis=0)
    give, sums_peer = tie(give, state["sums_peer"])
    got = over_dp(give, PERM_X).astype(F32)
    near_keep = (near_keep + got[:gu_part]).astype(BF)
    near_took = (near_took.astype(F32) + got[gu_part : 2 * gu_part]).astype(BF)
    grad_gate = pick(on_c0, near_keep[:, :half_ff], near_took[:, :half_ff], 1)
    grad_up = pick(on_c0, near_keep[:, half_ff:], near_took[:, half_ff:], 1)
    grad_down = unpack_down((down_mine + got[2 * gu_part :]).astype(BF), width)

    token_grad = summed(state["hot"], back[:, width:]) + sums_peer.astype(F32)
    token_grad = swapped(token_grad.astype(BF))

    return mixed, token_grad, grad_gate[None], grad_up[None], grad_down[None]


def solution(mesh):
    in_specs = (
        P(("dp", "expert"), None),
        P(("dp", "expert"), None),
        P(("dp", "expert"), None),
        P(("dp", "expert"), None),
        P("expert", "dp", None),
        P("expert", "dp", None),
        P("expert", "dp", None),
    )
    out_specs = (
        P(("dp", "expert"), None),
        P(("dp", "expert"), None),
        P("expert", "dp", None),
        P("expert", "dp", None),
        P("expert", "dp", None),
    )
    return jax.shard_map(shards, mesh=mesh, in_specs=in_specs, out_specs=out_specs, check_vma=False)
```

```python
import jax
import jax.numpy as jnp
from jax import lax
from jax.sharding import PartitionSpec as P

EXPERTS = 8
BLOCK = 64
N_X, N_Z, N_C = 2, 8, 2
N_L, N_Y = 2, 4
BF = jnp.bfloat16
F32 = jnp.float32


def dp_index(x, z, c):
    return (x * N_Z + z) * N_C + c


DP_ALL = [(x, z, c) for x in range(N_X) for z in range(N_Z) for c in range(N_C)]
PERM_UP = [(dp_index(x, z, c), dp_index(x, (z + 1) % N_Z, c)) for x, z, c in DP_ALL]
PERM_DOWN = [(dp_index(x, z, c), dp_index(x, (z - 1) % N_Z, c)) for x, z, c in DP_ALL]
PERM_CORE = [(dp_index(x, z, c), dp_index(x, z, 1 - c)) for x, z, c in DP_ALL]
PERM_X = [(dp_index(x, z, c), dp_index(1 - x, z, c)) for x, z, c in DP_ALL]
PERM_X_TO = [(dp_index(c, z, c), dp_index(1 - c, z, c)) for z in range(N_Z) for c in range(N_C)]
PERM_L = [(a * N_Y + y, (1 - a) * N_Y + y) for a in range(N_L) for y in range(N_Y)]


def perm_y(shift):
    return [(a * N_Y + y, a * N_Y + (y + shift) % N_Y) for a in range(N_L) for y in range(N_Y)]


def over_dp(value, perm):
    return lax.ppermute(value, "dp", perm)


def over_expert(value, perm):
    return lax.ppermute(value, "expert", perm)


def mm(a, b, dims=((1,), (0,))):
    return lax.dot_general(a, b, (dims, ((), ())), preferred_element_type=F32)


def put(buffer, part, z, row=0):
    return lax.dynamic_update_slice(buffer, part[None], (z, row, 0))


def ring_gather(slab, z, hooks):
    rows = slab.shape[0]
    half = rows // 2
    own = put(jnp.zeros((N_Z,) + slab.shape, slab.dtype), slab, z)
    up, down = slab, slab
    for step in range(1, 5):
        if step == 4:
            up, down = up[:half], down[half:]
        if step in hooks:
            up, down = hooks[step](up, down)
        up, down = tie(over_dp(up, PERM_UP), over_dp(down, PERM_DOWN))
        if step == 4:
            up, down = hooks[5](up, down)
        last = half if step == 4 else 0
        own = put(own, hooks["keep", step](up) if ("keep", step) in hooks else up, (z - step) % N_Z)
        own = put(own, down, (z + step) % N_Z, last)
    return own, over_dp(own, PERM_CORE)


def ring_scatter(partial_at, z, hooks):
    def at(step):
        return partial_at((z + step) % N_Z)

    def send(up, down):
        return tie(over_dp(up, PERM_UP), over_dp(down, PERM_DOWN))

    far = hooks[1](at(4))
    half = far.shape[0] // 2
    up, down = send(far[:half], far[half:])
    up = hooks[2](up)
    near_up, near_down = at(3), at(5)
    up = jnp.concatenate([near_up[:half] + up, near_up[half:]], axis=0)
    down = jnp.concatenate([near_down[:half], near_down[half:] + down], axis=0)
    up, down = send(up, down)
    up = hooks[3](up)
    up, down = send(at(2) + up, at(-2) + down)
    up = hooks[4](up)
    up, down = send(at(1) + up, at(-1) + down)
    return at(0).astype(F32) + up.astype(F32) + down.astype(F32)


def pack_down(d, ff):
    group = d.shape[-2] // 3
    last = [d[..., k * group : (k + 1) * group, 2 * ff :] for k in range(3)]
    last = jnp.concatenate(last, axis=-1)
    parts = [d[..., :ff], d[..., ff : 2 * ff], last[..., :ff], last[..., ff:]]
    return jnp.concatenate(parts, axis=-2)


def unpack_down(packed, width):
    ff = packed.shape[-1]
    group = packed.shape[-2] // 8
    short = width - 2 * ff
    last = jnp.concatenate([packed[..., 6 * group : 7 * group, :], packed[..., 7 * group :, :]], axis=-1)
    last = [last[..., k * short : (k + 1) * short] for k in range(3)]
    parts = [packed[..., : 3 * group, :], packed[..., 3 * group : 6 * group, :], jnp.concatenate(last, axis=-2)]
    return jnp.concatenate(parts, axis=-1)


def pick(first, a, b, axis):
    return jnp.where(first, jnp.concatenate([a, b], axis=axis), jnp.concatenate([b, a], axis=axis))


def four_blocks(rows):
    n = rows.shape[0] // N_Y
    return [rows[k * n : (k + 1) * n] for k in range(N_Y)]


def swap_near(blocks, sign):
    return over_expert(blocks[1], perm_y(sign)), over_expert(blocks[3], perm_y(-sign))


def swap_blocks(rows, sign, at_once):
    blocks = four_blocks(rows)
    one, three = swap_near(blocks, sign)
    two = blocks[2]
    if not at_once:
        one, two = tie(one, two)
    return [blocks[0], one, over_expert(two, perm_y(2)), three]


def tie(*values):
    return lax.optimization_barrier(values)


def slots_of(routes):
    tok_rows = routes.shape[0]
    experts = jnp.arange(EXPERTS, dtype=jnp.int32)
    onehot = (routes[:, :, None] == experts).astype(F32)
    named = jnp.sum(onehot, axis=1).astype(BF)
    earlier = jnp.arange(tok_rows)[:, None] > jnp.arange(tok_rows)[None, :]
    before = mm(earlier.astype(BF), named)
    return jnp.sum(onehot * before[:, None, :], axis=2)


def shards(tokens, routes, route_weights, cotangent, w_gate, w_up, w_down):
    tok_rows, width = tokens.shape
    ff = w_gate.shape[2]
    half_ff = ff // 2
    half_d = width // 2
    dp = lax.axis_index("dp")
    expert = lax.axis_index("expert")
    c, z, x = dp % N_C, (dp // N_C) % N_Z, dp // (N_C * N_Z)
    y, low = expert % N_Y, expert // N_Y
    on_c0, on_x0 = c == 0, x == 0

    wg, wu, wd = w_gate[0], w_up[0], w_down[0]

    def halves(k):
        return jnp.concatenate(
            [
                lax.dynamic_slice_in_dim(wg, k * half_ff, half_ff, 1),
                lax.dynamic_slice_in_dim(wu, k * half_ff, half_ff, 1),
            ],
            axis=1,
        )

    near = pick(on_c0, halves(c), over_dp(halves(1 - c), PERM_CORE), 0)
    down_pair = pick(on_c0, wd, over_dp(wd, PERM_CORE), 0)
    near, down_pair, routes = tie(near, down_pair, routes)
    far = over_dp(near, PERM_X)
    down_slab = jnp.where(x == c, down_pair, over_dp(down_pair, PERM_X_TO))

    packed = jnp.concatenate([routes.astype(F32).T, slots_of(routes).T, route_weights.T], axis=0)
    packed_peer = over_expert(packed, PERM_L)
    token_pair = jnp.concatenate([tokens, cotangent], axis=1)
    tokens_out, packed_peer = tie(tokens, packed_peer)
    tokens_peer = over_expert(tokens_out, PERM_L)

    def tables(info):
        numbers = jnp.arange(N_Y * BLOCK, dtype=jnp.int32)[:, None]
        hits, weights = [], []
        for j in range(2):
            ids = info[j].astype(jnp.int32)
            row = ((ids % N_Y - y) % N_Y) * BLOCK + info[2 + j].astype(jnp.int32)
            row = jnp.where(ids // N_Y == low, row, -1)
            hit = numbers == row[None, :]
            hits.append(hit.astype(F32))
            weights.append(jnp.where(hit, info[4 + j][None, :], 0.0))
        weight = weights[0] + weights[1]
        return (hits[0] + hits[1]).astype(BF), weight, jnp.sum(weight, axis=1, keepdims=True)

    def swapped(values):
        return pick(on_x0, values[:, :half_d], values[:, half_d:], 1)

    def dispatch(table, scale, pair, at_once):
        lanes = jnp.concatenate([swapped(pair[:, :width]), pair[:, width:]], axis=1)
        scales = jnp.where(jnp.arange(2 * width) < width, 1.0, scale)
        return swap_blocks((mm(table, lanes) * scales).astype(BF), 1, at_once)

    hot, weight, slot_weight = tables(packed)
    hot_peer, weight_peer, slot_weight_peer = tables(packed_peer)

    state = {"got": dispatch(hot, slot_weight, token_pair, False)}

    def keep_first(part):
        part, *state["got"] = tie(part, *state["got"])
        return part

    def before_second(up, down):
        up, down, tokens_in, cot_out = tie(up, down, tokens_peer, cotangent)
        state["cot"] = over_expert(cot_out, PERM_L)
        sent = mm(hot_peer, swapped(tokens_in)).astype(BF)
        *state["got"], sent = tie(*state["got"], sent)
        state["rows"] = four_blocks(sent)
        state["rows_near"] = swap_near(state["rows"], 1)
        return up, down

    def before_third(up, down):
        up, down, *state["rows_near"] = tie(up, down, *state["rows_near"])
        grads = four_blocks((mm(hot_peer, state["cot"]) * slot_weight_peer).astype(BF))
        state["two"] = over_expert(jnp.concatenate([state["rows"][2], grads[2]], axis=1), perm_y(2))
        state["grads_near"] = swap_near(grads, 1)
        state["grads"] = grads
        return up, down

    def after_fourth(up, down):
        up, down, state["two"], *state["grads_near"] = tie(up, down, state["two"], *state["grads_near"])
        return up, down

    slab = jnp.concatenate([near, far, pack_down(down_slab, ff)], axis=0)
    hooks = {
        2: before_second,
        3: before_third,
        5: after_fourth,
        ("keep", 1): keep_first,
    }
    own, other = ring_gather(slab, z, hooks)
    gu_rows = half_d // N_Z

    def weights(gathered):
        return (
            gathered[:, :gu_rows].reshape(half_d, ff),
            gathered[:, gu_rows : 2 * gu_rows].reshape(half_d, ff),
            unpack_down(gathered[:, 2 * gu_rows :], width).reshape(half_ff, width),
        )

    near_own, far_own, down_own = weights(own)
    near_oth, far_oth, down_oth = weights(other)

    (grads_one, grads_three), (rows_one, rows_three) = state["grads_near"], state["rows_near"]
    peer = [(state["rows"][0], state["grads"][0]), (rows_one, grads_one), (rows_three, grads_three)]
    peer = [jnp.concatenate(block, axis=1) for block in peer]
    got = jnp.concatenate([*state["got"], *peer[:2], state["two"], peer[2]], axis=0)
    rows, grads = got[:, :width], got[:, width:]
    rows_near, rows_far = rows[:, :half_d], rows[:, half_d:]

    def forward(w_near, w_far):
        both_values = mm(rows_near, w_near) + mm(rows_far, w_far)
        gate, up = both_values[:, :half_ff], both_values[:, half_ff:]
        sig = jax.nn.sigmoid(gate)
        return gate, up, sig, (gate * sig * up).astype(BF)

    gate_oth, up_oth, sig_oth, hid_oth = forward(near_oth, far_oth)
    gate_own, up_own, sig_own, hid_own = forward(near_own, far_own)

    def backward(gate, up, sig, w):
        hidden_grad = mm(grads, w, ((1,), (1,)))
        gate_grad = hidden_grad * up * sig * (1.0 + gate * (1.0 - sig))
        up_grad = hidden_grad * gate * sig
        return jnp.concatenate([gate_grad.astype(BF), up_grad.astype(BF)], axis=1)

    def over_rows(a, b):
        return mm(a, b, ((0,), (0,))).astype(BF)

    grad_oth = backward(gate_oth, up_oth, sig_oth, down_oth)
    grad_own = backward(gate_own, up_own, sig_own, down_own)

    def both_cores(left, own_half, other_half, rows_z):
        theirs = over_dp(over_rows(left[1], other_half), PERM_CORE)
        summed = over_rows(left[0], own_half) + theirs
        return summed.reshape(N_Z, rows_z, summed.shape[1])

    part_near = both_cores((rows_near, rows_near), grad_own, grad_oth, gu_rows)
    part_far = both_cores((rows_far, rows_far), grad_own, grad_oth, gu_rows)
    part_down = both_cores((hid_own, hid_oth), grads, grads, half_ff // N_Z)

    def partial_at(k):
        near_k, far_k, down_k = (
            lax.dynamic_index_in_dim(part, k, 0, keepdims=False)
            for part in (part_near, part_far, part_down)
        )
        return jnp.concatenate([near_k, far_k, pack_down(down_k, ff)], axis=0)

    def input_grad(own, oth):
        return (mm(grad_own, own, ((1,), (1,))) + mm(grad_oth, oth, ((1,), (1,)))).astype(BF)

    def weighted(weight, values):
        high = weight.astype(BF)
        rest = (weight - high.astype(F32)).astype(BF)
        return mm(high, values, ((0,), (0,))) + mm(rest, values, ((0,), (0,)))

    def summed(hot, values):
        return mm(hot, values, ((0,), (0,)))

    def before_first(value):
        output = (mm(hid_own, down_own) + mm(hid_oth, down_oth)).astype(BF)
        inputs = [input_grad(near_own, near_oth), input_grad(far_own, far_oth)]
        value, results = tie(value, jnp.concatenate([output, *inputs], axis=1))
        split = N_Y * BLOCK
        *got, home = tie(*swap_blocks(results[split:], -1, False), results[:split])
        state["back_peer"] = jnp.concatenate(got, axis=0)
        state["back"] = jnp.concatenate(swap_blocks(home, -1, False), axis=0)
        return value

    def before_third(value):
        value, late_weight, state["hot_peer"] = tie(value, weight_peer, hot_peer)
        mixed = weighted(late_weight, state["back_peer"][:, :width]).astype(BF)
        state["mixed_peer"] = over_expert(mixed, PERM_L)
        return value

    def before_fourth(value):
        sums = summed(state["hot_peer"], state["back_peer"][:, width:]).astype(BF)
        state["mixed_peer"], sums = tie(state["mixed_peer"], sums)
        state["sums_peer"] = over_expert(sums, PERM_L)
        value, state["hot"], state["weight"] = tie(value, hot, weight)
        return value

    hooks = {1: before_first, 2: lambda value: value, 3: before_third, 4: before_fourth}
    total = ring_scatter(partial_at, z, hooks)
    back = state["back"]
    mixed = weighted(state["weight"], back[:, :width]) + state["mixed_peer"].astype(F32)
    mixed = mixed.astype(BF)

    gu_part, down_part = gu_rows // 2, wd.shape[0]

    sum_down = unpack_down(total[4 * gu_part :], width)

    def rows_of(k):
        near_rows = lax.dynamic_slice_in_dim(total[: 2 * gu_part], k * gu_part, gu_part, 0)
        far_rows = lax.dynamic_slice_in_dim(total[2 * gu_part : 4 * gu_part], k * gu_part, gu_part, 0)
        down = lax.dynamic_slice_in_dim(sum_down, k * down_part, down_part, 0)
        return near_rows, far_rows, pack_down(down, ff)

    near_keep, far_keep, down_keep = rows_of(c)
    took = over_dp(jnp.concatenate(rows_of(1 - c), axis=0).astype(BF), PERM_CORE)
    near_took, far_took, down_took = jnp.split(took, [gu_part, 2 * gu_part], axis=0)
    down_took = down_took.astype(F32)
    down_mine = jnp.where(x == c, down_keep, down_took)
    down_give = jnp.where(x == c, down_took, down_keep).astype(BF)
    give = jnp.concatenate([far_keep.astype(BF), far_took, down_give], axis=0)
    give, sums_peer = tie(give, state["sums_peer"])
    got = over_dp(give, PERM_X).astype(F32)
    near_keep = (near_keep + got[:gu_part]).astype(BF)
    near_took = (near_took.astype(F32) + got[gu_part : 2 * gu_part]).astype(BF)
    grad_gate = pick(on_c0, near_keep[:, :half_ff], near_took[:, :half_ff], 1)
    grad_up = pick(on_c0, near_keep[:, half_ff:], near_took[:, half_ff:], 1)
    grad_down = unpack_down((down_mine + got[2 * gu_part :]).astype(BF), width)

    token_grad = summed(state["hot"], back[:, width:]) + sums_peer.astype(F32)
    token_grad = swapped(token_grad.astype(BF))

    return mixed, token_grad, grad_gate[None], grad_up[None], grad_down[None]


def solution(mesh):
    in_specs = (
        P(("dp", "expert"), None),
        P(("dp", "expert"), None),
        P(("dp", "expert"), None),
        P(("dp", "expert"), None),
        P("expert", "dp", None),
        P("expert", "dp", None),
        P("expert", "dp", None),
    )
    out_specs = (
        P(("dp", "expert"), None),
        P(("dp", "expert"), None),
        P("expert", "dp", None),
        P("expert", "dp", None),
        P("expert", "dp", None),
    )
    return jax.shard_map(shards, mesh=mesh, in_specs=in_specs, out_specs=out_specs, check_vma=False)
```
